128 devices in a mesh: bins: 4 (over z), tiles: 32 (over y, x, core).
Axes of the slice: x: 4, y: 4, z: 4, core: 2. Of those that a mesh axis runs over, the one named last changes fastest.
Arguments:
- spectrum: float32 [1800, 256, 256], P('bins', 'tiles'), may hold values from 0.1 to 2
- speed: float32 [50], replicated, may hold values from 0.3 to 0.95
- quad_a: bfloat16 [1800, 1800], replicated, may hold values from -0.125 to 0.125
- quad_b: bfloat16 [1800, 1800], replicated, may hold values from -0.125 to 0.125
- growth: float32 [1800], replicated, may hold values from 0.05 to 0.5
- dissip: float32 [1800], replicated, may hold values from 0.05 to 0.5
- wind: float32 [128, 512], P(('bins', 'tiles')), may hold values from 0.3 to 3
- cell_slot: int32 [256, 256], P('tiles'), may hold values from -1 to 2047, as said below
Outputs:
- evolved: float32 [1800, 256, 256], P('bins', 'tiles')
The draws below stay inside these ranges and needn't reach their ends.
Inputs may be any that keep to these rules, and one draw needn't show every extreme that they name: `cell_slot`: -1 on land; otherwise s * 16 + m, meaning that shard s holds this cell in slot m of the cell's tile; within one tile (rows t * 8 to t * 8 + 7) each value appears at most once, a shard's used slots of a tile are 0 up to some count, and some shard has all 16 slots used in every tile.
All inputs are finite; a program needn't handle non-finite values.
Results may differ from the reference program's by a relative error of at most 0.0011.
Values may be sent and summed in bfloat16 or wider, within the bound.
A program may use at most 128 MiB of HBM per device.

```python
import math
import jax
import jax.numpy as jnp
from jax import lax

ND = 36
NF = 50
NB = 1800
CX = 8
NY = 256
NX = 256
MOST = 16
SLOTS = 512
N_BINS = 4
N_TILES = 32
DEVICES = 128


def draw_cell_slot(key, part):
    base = jax.random.fold_in(key, 7)
    key_count, key_full, key_perm = jax.random.split(base, 3)
    devices = N_BINS * N_TILES
    cells = CX * NY
    counts = jax.random.randint(key_count, (N_TILES, devices), MOST // 4, MOST + 1)
    full = jax.random.randint(key_full, (), 0, devices)
    counts = jnp.where(jnp.arange(devices)[None, :] == full, MOST, counts).astype(jnp.int32)
    starts = jnp.cumsum(counts, axis=1) - counts
    perms = jax.vmap(lambda sub: jax.random.permutation(sub, cells))(jax.random.split(key_perm, N_TILES)).astype(jnp.int32)
    places = jnp.arange(MOST, dtype=jnp.int32)
    position = starts[:, :, None] + places[None, None, :]
    valid = places[None, None, :] < counts[:, :, None]
    position = jnp.clip(position, 0, cells - 1).reshape(N_TILES, devices * MOST)
    picked = jnp.take_along_axis(perms, position, axis=1).reshape(N_TILES, devices, MOST)
    sends = jnp.where(valid, picked, -1).astype(jnp.int32)
    values = jnp.arange(devices, dtype=jnp.int32)[:, None] * MOST + places[None, :]
    values = jnp.broadcast_to(values[None], sends.shape)
    tile_rows = jnp.broadcast_to(jnp.arange(N_TILES, dtype=jnp.int32)[:, None, None], sends.shape)
    columns = jnp.where(valid, sends, cells)
    table = jnp.full((N_TILES, cells), -1, jnp.int32).at[tile_rows, columns].set(values, mode='drop')
    return table.reshape(N_TILES * CX, NY)


def shard_levels(rng, dims, cuts, low, high):
    gain, own = 1.0, jax.random.fold_in(rng, 6)
    for axis_at, blocks in cuts:
        steps = jnp.exp(jax.random.uniform(jax.random.fold_in(own, axis_at), (blocks,), jnp.float32, low / len(cuts), high / len(cuts)))
        gain = gain * jnp.repeat(steps, dims[axis_at] // blocks).reshape([-1 if axis == axis_at else 1 for axis in range(len(dims))])
    return gain


def gaussian(stream_key, dims, spread, reach, kind=jnp.bfloat16):
    drawn = jax.random.normal(stream_key, dims, jnp.float32) * spread
    return jnp.minimum(jnp.maximum(drawn, -reach), reach).astype(kind)


def setup_inputs(seed: int = 0) -> dict:
    seeds = jax.random.split(jax.random.key(seed), 9)
    spectrum = jnp.clip(jnp.exp(math.log(2.0) - 2.9957323 * jax.random.uniform(seeds[0], (NB, NX, NY), jnp.float32) ** shard_levels(seeds[0], (NB, NX, NY), ((0, 4), (1, 32)), -0.2, 0.2)), 0.1, 2.0)
    speed = jnp.clip(jax.random.uniform(seeds[1], (NF,), jnp.float32, 0.3, 0.95), 0.3, 0.95)
    quad_a = gaussian(seeds[2], (NB, NB), NB ** -0.5, 0.125)
    quad_b = gaussian(seeds[3], (NB, NB), NB ** -0.5, 0.125)
    growth = jnp.clip(jnp.exp(jax.random.uniform(seeds[4], (NB,), jnp.float32, math.log(0.05), math.log(0.5))), 0.05, 0.5)
    dissip = jnp.clip(jnp.exp(jax.random.uniform(seeds[5], (NB,), jnp.float32, math.log(0.05), math.log(0.5))), 0.05, 0.5)
    wind = jnp.clip(jnp.exp(math.log(3.0) - 2.3025851 * jax.random.uniform(seeds[6], (DEVICES, SLOTS), jnp.float32) ** shard_levels(seeds[6], (DEVICES, SLOTS), ((0, 128),), -0.2, 0.2)), 0.3, 3.0)
    cell_slot = draw_cell_slot(jax.random.fold_in(seeds[8], 71), 0)
    return {"spectrum": spectrum, "speed": speed, "quad_a": quad_a, "quad_b": quad_b, "growth": growth, "dissip": dissip, "wind": wind, "cell_slot": cell_slot}


time_step = 0.25


def courant(bins, speed, nfreq, ndir):
    direction = bins // nfreq
    freq = bins % nfreq
    theta = (direction.astype(jnp.float32) + 0.5) * (2.0 * math.pi / ndir)
    cosine = jnp.cos(theta)
    sine = jnp.sin(theta)
    total = jnp.abs(cosine) + jnp.abs(sine)
    rate = speed[freq]
    return rate * cosine / total, rate * sine / total


def advance(field, west, east, cour_x, cour_y, sea):
    cxb = cour_x[:, None, None]
    cyb = cour_y[:, None, None]
    ypad = jnp.pad(field, ((0, 0), (0, 0), (1, 1)))
    south = ypad[:, :, :-2]
    north = ypad[:, :, 2:]
    up_x = jnp.where(cxb > 0, west, east)
    up_y = jnp.where(cyb > 0, south, north)
    return (field - jnp.abs(cxb) * (field - up_x) - jnp.abs(cyb) * (field - up_y)) * sea


def reference(spectrum, speed, quad_a, quad_b, growth, dissip, wind, cell_slot):
    sea = (cell_slot >= 0).astype(jnp.float32)
    field = spectrum * sea[None]
    bins = jnp.arange(NB, dtype=jnp.int32)
    cour_x, cour_y = courant(bins, speed, NF, ND)
    xpad = jnp.pad(field, ((0, 0), (1, 1), (0, 0)))
    prop = advance(field, xpad[:, :-2], xpad[:, 2:], cour_x, cour_y, sea[None])
    sent = prop.astype(jnp.bfloat16)
    tile_of = (jnp.arange(NX, dtype=jnp.int32) // CX)[:, None]
    shard = cell_slot // MOST
    within = cell_slot % MOST
    widx = jnp.where(cell_slot >= 0, shard * SLOTS + tile_of * MOST + within, 0).astype(jnp.int32)
    wind_cell = wind.reshape(-1)[widx]
    sent_t = sent.reshape(NB, N_TILES, CX * NY).transpose(1, 0, 2)
    wind_t = wind_cell.reshape(N_TILES, CX * NY)
    qa_t = quad_a.astype(jnp.float32).T
    qb_t = quad_b.astype(jnp.float32).T

    def one_tile(pair):
        energy = pair[0].astype(jnp.float32)
        force = pair[1]
        pair_a = jnp.dot(qa_t, energy, precision=lax.Precision.HIGHEST)
        pair_b = jnp.dot(qb_t, energy, precision=lax.Precision.HIGHEST)
        mean_e = jnp.sum(energy, axis=0) / NB
        total = pair_a * pair_b + growth[:, None] * force[None, :] * energy - dissip[:, None] * mean_e[None, :] * energy
        return (time_step * total).astype(jnp.bfloat16)

    change = lax.map(one_tile, (sent_t, wind_t))
    change = change.transpose(1, 0, 2).reshape(NB, NX, NY)
    return prop + change.astype(jnp.float32) * sea[None]
```

```python
import functools
import math

import jax
import jax.numpy as jnp
import numpy as np
from jax import lax
from jax.experimental import pallas as pl
from jax.experimental.pallas import tpu as pltpu
from jax.sharding import PartitionSpec as P

MESH = pl.DeviceIdType.MESH
F32 = jnp.float32
BF16 = jnp.bfloat16

GROUPS = 4
TILES = 32
OWN = 450
STEP = 448
WIN = 464
BINS = 1800
ROWS = 8
COLS = 256
CELLS = 2 * COLS
MOST = 16
SUB = 16
NT = (((1,), (1,)), ((), ()))


def kernel(
    cap,
    parts,
    spec,
    quad_a,
    quad_b,
    coef,
    wind,
    slot,
    out,
    most,
    field,
    qa,
    qb,
    sea,
    place,
    onehot,
    halo_out,
    halo_in,
    prop,
    sent,
    ahead,
    held,
    heldt,
    pairs,
    pairst,
    back,
    got,
    inc,
    wp,
    wy,
    wx,
    wc,
    wz,
    table,
    load_sem,
    halo_sem,
    fwd_send,
    fwd_recv,
    ret_send,
    ret_recv,
    wind_send,
    wind_recv,
):
    z = lax.axis_index("bins")
    t = lax.axis_index("tiles")
    ty = t // 8
    tx = (t // 2) % 4
    tc = t % 2
    west = 1 - ((z + 1) // 2) % 2
    turn = 2 * west - 1
    count = WIN // SUB

    for h in range(2):
        field[h, 0:8] = jnp.zeros((8, ROWS, 128), F32)
        field[h, STEP:WIN] = jnp.zeros((WIN - STEP, ROWS, 128), F32)
    load_x = [
        pltpu.make_async_copy(
            spec.at[:, :, pl.ds(128 * h, 128)], field.at[h, pl.ds(2 * z, OWN)], load_sem.at[h]
        )
        for h in range(2)
    ]
    for load in load_x:
        load.start()
    load_a = pltpu.make_async_copy(quad_a, qa, load_sem.at[2])
    load_b = pltpu.make_async_copy(quad_b, qb, load_sem.at[3])
    load_a.start()
    load_b.start()

    barrier = pltpu.get_barrier_semaphore()
    peers = [(lax.rem(z + i, 4), t) for i in (1, 2, 3)]
    peers += [(z, lax.rem(t + 1, TILES)), (z, lax.rem(t + TILES - 1, TILES))]
    ypeers = [lax.rem(ty + i, 4) for i in (1, 2, 3)]
    xpeers = [lax.rem(tx + i, 4) for i in (1, 2, 3)]
    peers += [(z, p * 8 + lax.rem(t, 8)) for p in ypeers]
    peers += [(z, ty * 8 + p * 2 + tc) for p in xpeers]
    for peer in peers:
        pl.semaphore_signal(barrier, inc=1, device_id=peer, device_id_type=MESH)

    wet = (slot[...] >= 0).astype(F32)
    sea[...] = wet
    left = lax.broadcasted_iota(jnp.int32, (COLS, COLS), 0)
    right = lax.broadcasted_iota(jnp.int32, (COLS, COLS), 1)
    upto = (left <= right).astype(F32).astype(BF16)
    running = jnp.dot(wet.astype(BF16), upto, preferred_element_type=F32)
    total = jnp.sum(wet, axis=1, keepdims=True)
    before = pltpu.roll(jnp.broadcast_to(total, (ROWS, COLS)), 1, 0)
    odd = lax.broadcasted_iota(jnp.int32, (ROWS, COLS), 0) % 2 == 1
    running = running + jnp.where(odd, before, 0.0)
    place[...] = jnp.where(wet > 0, running - 1.0, -1.0)
    fullest = jnp.max(running)

    held[:, WIN:512, :] = jnp.zeros((GROUPS, 512 - WIN, cap), BF16)
    pairs[:, 1792:1920] = jnp.zeros((pairs.shape[0], 128), BF16)

    flat = field.reshape(2 * WIN * ROWS, 128)

    def strip(i, r):
        base = i * (SUB * ROWS) + r
        return [pl.ds(h * (WIN * ROWS) + base, SUB, stride=ROWS) for h in range(2)]

    def take(i, r):
        return jnp.concatenate([flat[at, :] for at in strip(i, r)], axis=1)

    def put(i, r, value):
        for h, at in enumerate(strip(i, r)):
            flat[at, :] = value[:, 128 * h : 128 * h + 128]

    for load in load_x:
        load.wait()
    edge = 7 * west
    edge_sea = sea[pl.ds(edge, 1), :]

    def halo_step(i, carry):
        v = take(i, edge)
        halo_out[pl.ds(pl.multiple_of(i * SUB, SUB), SUB), :] = v * edge_sea
        return carry

    lax.fori_loop(0, count, halo_step, 0)
    pl.semaphore_wait(barrier, len(peers))
    halo = pltpu.make_async_remote_copy(
        src_ref=halo_out,
        dst_ref=halo_in,
        send_sem=halo_sem.at[0],
        recv_sem=halo_sem.at[1],
        device_id=(z, lax.rem(t + turn + TILES, TILES)),
        device_id_type=MESH,
    )
    halo.start()
    outer = (1 - west) * (TILES - 1)
    halo_there = (t != outer).astype(F32)

    lane = lax.broadcasted_iota(jnp.int32, (SUB, COLS), 1)
    south = z < 2
    shift = jnp.where(south, 1, COLS - 1)
    wall = lane == jnp.where(south, 0, COLS - 1)
    from_west = west == 1

    def propagate(g, edged):
        r0 = 2 * g
        ru = jnp.clip(r0 + 2 - 3 * west, 0, ROWS - 1)
        sea0 = sea[pl.ds(r0, 1), :]
        sea1 = sea[pl.ds(r0 + 1, 1), :]
        seau = sea[pl.ds(ru, 1), :]
        at_edge = g == (1 - west) * (GROUPS - 1)

        def step(i, carry):
            here = pl.ds(pl.multiple_of(i * SUB, SUB), SUB)
            f0 = take(i, r0) * sea0
            f1 = take(i, r0 + 1) * sea1
            fu = take(i, ru) * seau
            if edged:
                fu = jnp.where(at_edge, halo_in[here, :] * halo_there, fu)
            consts = coef[pl.ds(pl.multiple_of(z * STEP + i * SUB, SUB), SUB), :]
            cx = consts[:, 0:1]
            cy = consts[:, 1:2]
            up0 = jnp.where(from_west, fu, f1)
            up1 = jnp.where(from_west, f0, fu)
            y0 = jnp.where(wall, 0.0, pltpu.roll(f0, shift, 1))
            y1 = jnp.where(wall, 0.0, pltpu.roll(f1, shift, 1))
            p0 = (f0 - cx * (f0 - up0) - cy * (f0 - y0)) * sea0
            p1 = (f1 - cx * (f1 - up1) - cy * (f1 - y1)) * sea1
            prop[g, here, 0:COLS] = p0
            prop[g, here, COLS:CELLS] = p1
            sent[here, 0:COLS] = p0.astype(BF16)
            sent[here, COLS:CELLS] = p1.astype(BF16)
            return carry

        lax.fori_loop(0, count, step, 0)
        rank = lax.broadcasted_iota(jnp.int32, (cap, COLS), 0).astype(F32)
        onehot[g, :, 0:COLS] = jnp.where(rank == place[pl.ds(r0, 1), :], 1.0, 0.0).astype(BF16)
        onehot[g, :, COLS:CELLS] = jnp.where(rank == place[pl.ds(r0 + 1, 1), :], 1.0, 0.0).astype(BF16)
        return lax.dot_general(sent[...], onehot[g], NT, preferred_element_type=F32).astype(BF16)

    late = z // 3
    order = [
        1 + lax.rem(z, 2),
        2 * (1 - (z + 2) // 3) + late,
        3 * (1 - late),
        z,
    ]

    starts = [sum(parts[:i]) for i in range(len(parts))]

    def forward(i, c):
        return pltpu.make_async_remote_copy(
            src_ref=ahead.at[i, :, pl.ds(starts[c], parts[c])],
            dst_ref=held.at[z, pl.ds(0, WIN), pl.ds(starts[c], parts[c])],
            send_sem=fwd_send.at[c, i],
            recv_sem=fwd_recv.at[c, z],
            device_id=(order[i], t),
            device_id_type=MESH,
        )

    for i in range(3):
        if i == 2:
            halo.wait()
        ahead[i] = propagate(order[i], i == 2)
        forward(i, 0).start()
    for c in range(1, len(parts)):
        for i in range(3):
            forward(i, c).start()
    held[z, 0:WIN, :] = propagate(z, True)

    mark = lax.broadcasted_iota(jnp.int32, (1, 128), 1)
    for p in range(TILES):
        row = wind[:, 128 * (p // 8) : 128 * (p // 8) + 128]
        if p % 8:
            row = pltpu.roll(row, 128 - MOST * (p % 8), 1)
        wp[p // 8, (p // 2) % 4, p % 2] = jnp.where(mark == MOST, fullest, row)
    wy[ty] = wp[ty]

    def wind_copy(k, src, dst, there):
        return pltpu.make_async_remote_copy(
            src_ref=src,
            dst_ref=dst,
            send_sem=wind_send.at[k],
            recv_sem=wind_recv.at[k],
            device_id=there,
            device_id_type=MESH,
        )

    def wind_y():
        return [
            wind_copy(i, wp.at[p], wy.at[ty], (z, p * 8 + lax.rem(t, 8))) for i, p in enumerate(ypeers)
        ]

    def wind_x():
        return [
            wind_copy(3 + i, wy.at[:, p], wx.at[tx], (z, ty * 8 + p * 2 + tc)) for i, p in enumerate(xpeers)
        ]

    def wind_c():
        return [wind_copy(6, wx.at[:, :, 1 - tc], wc.at[tc], (z, t + 1 - 2 * tc))]

    def wind_z():
        return [
            wind_copy(7 + i, wc, wz.at[z], (lax.rem(z + 1 + i, 4), t)) for i in range(3)
        ]

    def wind_next(stage):
        if stage == 0:
            for copy in wind_y():
                copy.start()
        if stage == 1:
            for copy in wind_y():
                copy.wait()
            wx[tx] = wy[:, tx]
            for copy in wind_x():
                copy.start()
        if stage == 2:
            for copy in wind_x():
                copy.wait()
            wc[tc] = wx[:, :, tc]
            for copy in wind_c():
                copy.start()
        if stage == 3:
            for copy in wind_c():
                copy.wait()
            wz[z] = wc[...]
            for copy in wind_z():
                copy.start()
        if stage == 4:
            for copy in wind_z():
                copy.wait()
            for i in range(128):
                table[i : i + 1, :] = wz[i // 32, (i // 16) % 2, (i // 4) % 4, i % 4]

    wind_next(0)

    load_a.wait()
    load_b.wait()

    def returning(i, c):
        h = lax.rem(z + i + 1, 4)
        return pltpu.make_async_remote_copy(
            src_ref=back.at[h, :, pl.ds(starts[c], parts[c])],
            dst_ref=got.at[z, :, pl.ds(starts[c], parts[c])],
            send_sem=ret_send.at[c, i],
            recv_sem=ret_recv.at[c, z],
            device_id=(h, t),
            device_id_type=MESH,
        )

    def landing(c, i):
        g = lax.rem(z + i + 1, 4)
        return pltpu.make_async_remote_copy(
            src_ref=ahead.at[i, :, pl.ds(starts[c], parts[c])],
            dst_ref=held.at[g, pl.ds(0, WIN), pl.ds(starts[c], parts[c])],
            send_sem=fwd_send.at[c, i],
            recv_sem=fwd_recv.at[c, g],
            device_id=(g, t),
            device_id_type=MESH,
        )

    def homing(c, i):
        g = lax.rem(z + i + 1, 4)
        return pltpu.make_async_remote_copy(
            src_ref=back.at[g, :, pl.ds(starts[c], parts[c])],
            dst_ref=got.at[g, :, pl.ds(starts[c], parts[c])],
            send_sem=ret_send.at[c, i],
            recv_sem=ret_recv.at[c, g],
            device_id=(g, t),
            device_id_type=MESH,
        )

    for c, n in enumerate(parts):
        at = pl.ds(starts[c], n)
        for i in range(3):
            landing(c, i).wait_recv()
        wind_next(1 + c)
        ones = jnp.ones((SUB, 512), BF16)
        mean = jnp.zeros((SUB, n), F32)
        for s in range(GROUPS):
            block = held[s, :, starts[c] : starts[c] + n]
            mean = mean + jnp.dot(ones, block, preferred_element_type=F32)
            heldt[0:n, 512 * s : 512 * s + 512] = block.T
        mean = mean / BINS
        for k0 in range(0, BINS, 512):
            k1 = min(k0 + 512, BINS)
            sums = []
            for q in (qa, qb):
                acc = None
                for s in range(GROUPS):
                    deep = min(WIN, BINS - STEP * s)
                    term = jnp.dot(
                        heldt[0:n, 512 * s : 512 * s + deep],
                        q[STEP * s : STEP * s + deep, k0:k1],
                        preferred_element_type=F32,
                    )
                    acc = term if acc is None else acc + term
                sums.append(acc)
            pairs[0:n, k0:k1] = (0.25 * (sums[0] * sums[1])).astype(BF16)
        for j in range(15):
            pairst[128 * j : 128 * j + 128, 0:n] = pairs[0:n, 128 * j : 128 * j + 128].T
        row = lax.broadcasted_iota(jnp.int32, (SUB, n), 0)
        high = mean.astype(BF16).astype(F32)
        mid = (mean - high).astype(BF16).astype(F32)
        low = mean - high - mid
        for h in range(GROUPS):
            back[h, 0:STEP, at] = pairst[STEP * h : STEP * h + STEP, 0:n]
            tail = pairst[STEP * h + STEP : STEP * h + WIN, 0:n].astype(F32)
            tail = jnp.where(row == 8, high, tail)
            tail = jnp.where(row == 9, mid, tail)
            tail = jnp.where(row == 10, low, tail)
            back[h, STEP:WIN, at] = tail.astype(BF16)
        for i in range(3):
            returning(i, c).start()

    for stage in range(1 + len(parts), 5):
        wind_next(stage)
    most[...] = jnp.broadcast_to(jnp.max(table[:, MOST : MOST + 1]), (8, 128))

    wide = table[...]
    w_high = wide.astype(BF16)
    w_mid = (wide - w_high.astype(F32)).astype(BF16)
    w_low = (wide - w_high.astype(F32) - w_mid.astype(F32)).astype(BF16)
    eye = (
        lax.broadcasted_iota(jnp.int32, (MOST, 128), 0) == lax.broadcasted_iota(jnp.int32, (MOST, 128), 1)
    ).astype(F32).astype(BF16)
    tables = [
        lax.dot_general(eye, w, NT, preferred_element_type=F32).astype(BF16) for w in (w_high, w_mid, w_low)
    ]

    def wind_row(r):
        cells = slot[pl.ds(r, 1), :]
        shard = cells // MOST
        line = (shard // 32) * 32 + (shard % 2) * 16 + ((shard // 2) % 4) * 4 + (shard // 8) % 4
        pick = lax.broadcasted_iota(jnp.int32, (128, COLS), 0) == line
        pick = jnp.where(pick, 1.0, 0.0).astype(BF16)
        found = sum(jnp.dot(w, pick, preferred_element_type=F32) for w in tables)
        here = lax.broadcasted_iota(jnp.int32, (MOST, COLS), 0) == cells % MOST
        return jnp.sum(jnp.where(here, found, 0.0), axis=0, keepdims=True)

    def finish(g, source):
        r0 = 2 * g
        inc[...] = jnp.dot(source[g], onehot[g], preferred_element_type=F32)
        means = jnp.sum(inc[STEP + 8 : STEP + 11, :], axis=0, keepdims=True)
        m0 = means[:, 0:COLS]
        m1 = means[:, COLS:CELLS]
        w0 = wind_row(r0)
        w1 = wind_row(r0 + 1)

        def step(i, carry):
            here = pl.ds(pl.multiple_of(i * SUB, SUB), SUB)
            consts = coef[pl.ds(pl.multiple_of(z * STEP + i * SUB, SUB), SUB), :]
            grow = consts[:, 2:3]
            damp = consts[:, 3:4]
            p0 = prop[g, here, 0:COLS]
            p1 = prop[g, here, COLS:CELLS]
            s0 = p0.astype(BF16).astype(F32)
            s1 = p1.astype(BF16).astype(F32)
            e0 = p0 + inc[here, 0:COLS] + (grow * w0 - damp * m0) * s0
            e1 = p1 + inc[here, COLS:CELLS] + (grow * w1 - damp * m1) * s1
            put(i, r0, e0)
            put(i, r0 + 1, e1)
            return carry

        lax.fori_loop(0, count, step, 0)

    finish(z, back)
    for i in range(3):
        for c in range(len(parts)):
            homing(c, i).wait_recv()
        finish(lax.rem(z + i + 1, 4), got)
    stores = [
        pltpu.make_async_copy(
            field.at[h, pl.ds(2 * z, OWN)], out.at[:, :, pl.ds(128 * h, 128)], load_sem.at[h]
        )
        for h in range(2)
    ]
    for store in stores:
        store.start()
    for i in range(3):
        for c in range(len(parts)):
            forward(i, c).wait_send()
            returning(i, c).wait_send()
    for store in stores:
        store.wait()


def coupled(cap, parts, cid, spectrum, quad_a, quad_b, coef, wind, slot):
    vmem = pl.BlockSpec(memory_space=pltpu.VMEM)
    hbm = pl.BlockSpec(memory_space=pl.ANY)
    n = len(parts)
    wide = max(parts)
    dma = pltpu.SemaphoreType.DMA
    return pl.pallas_call(
        functools.partial(kernel, cap, parts),
        out_shape=[
            jax.ShapeDtypeStruct(spectrum.shape, F32),
            jax.ShapeDtypeStruct((8, 128), F32),
        ],
        in_specs=[hbm, hbm, hbm, vmem, vmem, vmem],
        out_specs=[hbm, vmem],
        scratch_shapes=[
            pltpu.VMEM((2, WIN, ROWS, 128), F32),
            pltpu.VMEM((BINS, BINS), BF16),
            pltpu.VMEM((BINS, BINS), BF16),
            pltpu.VMEM((ROWS, COLS), F32),
            pltpu.VMEM((ROWS, COLS), F32),
            pltpu.VMEM((GROUPS, cap, CELLS), BF16),
            pltpu.VMEM((WIN, COLS), F32),
            pltpu.VMEM((WIN, COLS), F32),
            pltpu.VMEM((GROUPS, WIN, CELLS), F32),
            pltpu.VMEM((WIN, CELLS), BF16),
            pltpu.VMEM((3, WIN, cap), BF16),
            pltpu.VMEM((GROUPS, 512, cap), BF16),
            pltpu.VMEM((wide, GROUPS * 512), BF16),
            pltpu.VMEM((wide, 1920), BF16),
            pltpu.VMEM((1920, wide), BF16),
            pltpu.VMEM((GROUPS, WIN, cap), BF16),
            pltpu.VMEM((GROUPS, WIN, cap), BF16),
            pltpu.VMEM((WIN, CELLS), F32),
            pltpu.VMEM((4, 4, 2, 1, 128), F32),
            pltpu.VMEM((4, 4, 2, 1, 128), F32),
            pltpu.VMEM((4, 4, 2, 1, 128), F32),
            pltpu.VMEM((2, 4, 4, 1, 128), F32),
            pltpu.VMEM((4, 2, 4, 4, 1, 128), F32),
            pltpu.VMEM((128, 128), F32),
            dma((4,)),
            dma((2,)),
            dma((n, 3)),
            dma((n, 4)),
            dma((n, 3)),
            dma((n, 4)),
            dma((10,)),
            dma((10,)),
        ],
        compiler_params=pltpu.CompilerParams(
            collective_id=cid, has_side_effects=True, vmem_limit_bytes=56 << 20
        ),
        name="coupled%d" % cap,
    )(spectrum, quad_a, quad_b, coef, wind, slot)


def directions():
    theta = (np.arange(36) + 0.5) * (2.0 * math.pi / 36)
    cosine = np.abs(np.cos(theta))
    sine = np.abs(np.sin(theta))
    return cosine / (cosine + sine), sine / (cosine + sine)


def on_device(spectrum, speed, quad_a, quad_b, growth, dissip, wind, cell_slot):
    along, across = directions()
    cx = (jnp.asarray(along, F32)[:, None] * speed[None, :]).reshape(BINS)
    cy = (jnp.asarray(across, F32)[:, None] * speed[None, :]).reshape(BINS)
    coef = jnp.stack([cx, cy, 0.25 * growth, 0.25 * dissip], axis=1)
    coef = jnp.pad(coef, ((0, 8), (0, 0)))
    out, most = coupled(512, (256, 256), 0, spectrum, quad_a, quad_b, coef, wind, cell_slot)
    return out


def solution(mesh):
    placed = (
        P("bins", "tiles", None),
        P(),
        P(),
        P(),
        P(),
        P(),
        P(("bins", "tiles"), None),
        P("tiles", None),
    )
    return jax.shard_map(
        on_device, mesh=mesh, in_specs=placed, out_specs=P("bins", "tiles", None), check_vma=False
    )
```

```python
import functools
import math

import jax
import jax.numpy as jnp
from jax import lax
from jax.experimental import pallas as pl
from jax.experimental.pallas import tpu as pltpu
from jax.sharding import PartitionSpec as P

MESH = pl.DeviceIdType.MESH
F32 = jnp.float32
BF16 = jnp.bfloat16

GROUPS = 4
TILES = 32
OWN = 450
STEP = 448
WIN = 464
BINS = 1800
ROWS = 8
COLS = 256
CELLS = 2 * COLS
MOST = 16
SUB = 16
NT = (((1,), (1,)), ((), ()))


def kernel(
    cap,
    parts,
    spec,
    quad_a,
    quad_b,
    speed,
    growth,
    dissip,
    wind,
    slot,
    out,
    most,
    field,
    qa,
    qb,
    sea,
    place,
    onehot,
    rates,
    coef,
    halo_out,
    halo_in,
    prop,
    sent,
    ahead,
    held,
    heldt,
    pairs,
    pairst,
    back,
    got,
    inc,
    wp,
    wy,
    wx,
    wc,
    wz,
    table,
    load_sem,
    halo_sem,
    fwd_send,
    fwd_recv,
    ret_send,
    ret_recv,
    wind_send,
    wind_recv,
):
    z = lax.axis_index("bins")
    t = lax.axis_index("tiles")
    ty = t // 8
    tx = (t // 2) % 4
    tc = t % 2
    west = 1 - ((z + 1) // 2) % 2
    turn = 2 * west - 1
    count = WIN // SUB

    for h in range(2):
        field[h, 0:8] = jnp.zeros((8, ROWS, 128), F32)
        field[h, STEP:WIN] = jnp.zeros((WIN - STEP, ROWS, 128), F32)
    load_x = [
        pltpu.make_async_copy(
            spec.at[:, :, pl.ds(128 * h, 128)], field.at[h, pl.ds(2 * z, OWN)], load_sem.at[h]
        )
        for h in range(2)
    ]
    for load in load_x:
        load.start()
    load_a = pltpu.make_async_copy(quad_a, qa, load_sem.at[2])
    load_b = pltpu.make_async_copy(quad_b, qb, load_sem.at[3])
    barrier = pltpu.get_barrier_semaphore()
    peers = [(lax.rem(z + i, 4), t) for i in (1, 2, 3)]
    peers += [(z, lax.rem(t + 1, TILES)), (z, lax.rem(t + TILES - 1, TILES))]
    ypeers = [lax.rem(ty + i, 4) for i in (1, 2, 3)]
    xpeers = [lax.rem(tx + i, 4) for i in (1, 2, 3)]
    peers += [(z, p * 8 + lax.rem(t, 8)) for p in ypeers]
    peers += [(z, ty * 8 + p * 2 + tc) for p in xpeers]
    for peer in peers:
        pl.semaphore_signal(barrier, inc=1, device_id=peer, device_id_type=MESH)

    wet = (slot[...] >= 0).astype(F32)
    sea[...] = wet
    left = lax.broadcasted_iota(jnp.int32, (COLS, COLS), 0)
    right = lax.broadcasted_iota(jnp.int32, (COLS, COLS), 1)
    upto = (left <= right).astype(F32).astype(BF16)
    running = jnp.dot(wet.astype(BF16), upto, preferred_element_type=F32)
    total = jnp.sum(wet, axis=1, keepdims=True)
    before = pltpu.roll(jnp.broadcast_to(total, (ROWS, COLS)), 1, 0)
    odd = lax.broadcasted_iota(jnp.int32, (ROWS, COLS), 0) % 2 == 1
    running = running + jnp.where(odd, before, 0.0)
    place[...] = jnp.where(wet > 0, running - 1.0, -1.0)
    fullest = jnp.max(running)

    held[:, WIN:512, :] = jnp.zeros((GROUPS, 512 - WIN, cap), BF16)
    pairs[:, 1792:1920] = jnp.zeros((pairs.shape[0], 128), BF16)

    flat = field.reshape(2 * WIN * ROWS, 128)

    def strip(i, r):
        base = i * (SUB * ROWS) + r
        return [pl.ds(h * (WIN * ROWS) + base, SUB, stride=ROWS) for h in range(2)]

    def take(i, r):
        return jnp.concatenate([flat[at, :] for at in strip(i, r)], axis=1)

    def put(i, r, value):
        for h, at in enumerate(strip(i, r)):
            flat[at, :] = value[:, 128 * h : 128 * h + 128]

    def both(k, i):
        one = coef[k, pl.ds(pl.multiple_of(64 + i * SUB, SUB), SUB), :]
        return jnp.concatenate([one, one], axis=1)

    mark = lax.broadcasted_iota(jnp.int32, (1, 128), 1)
    for p in range(TILES):
        row = wind[:, 128 * (p // 8) : 128 * (p // 8) + 128]
        if p % 8:
            row = pltpu.roll(row, 128 - MOST * (p % 8), 1)
        wp[p // 8, (p // 2) % 4, p % 2] = jnp.where(mark == MOST, fullest, row)
    wz[z] = wp[...]

    def wind_copy(k, src, dst, there):
        return pltpu.make_async_remote_copy(
            src_ref=src,
            dst_ref=dst,
            send_sem=wind_send.at[k],
            recv_sem=wind_recv.at[k],
            device_id=there,
            device_id_type=MESH,
        )

    def wind_z():
        return [wind_copy(i, wp, wz.at[z], (lax.rem(z + 1 + i, 4), t)) for i in range(3)]

    def wind_y():
        return [
            wind_copy(3 + i, wz.at[:, p], wy.at[ty], (z, p * 8 + lax.rem(t, 8)))
            for i, p in enumerate(ypeers)
        ]

    def wind_x():
        return [
            wind_copy(6 + i, wy.at[:, :, p], wx.at[tx], (z, ty * 8 + p * 2 + tc))
            for i, p in enumerate(xpeers)
        ]

    def wind_c():
        return [wind_copy(9, wx.at[:, :, :, 1 - tc], wc.at[tc], (z, t + 1 - 2 * tc))]

    def wind_next(stage):
        if stage == 0:
            for copy in wind_z():
                copy.start()
        if stage == 1:
            for copy in wind_z():
                copy.wait()
            wy[ty] = wz[:, ty]
            for copy in wind_y():
                copy.start()
        if stage == 2:
            for copy in wind_y():
                copy.wait()
            wx[tx] = wy[:, :, tx]
            for copy in wind_x():
                copy.start()
        if stage == 3:
            for copy in wind_x():
                copy.wait()
            wc[tc] = wx[:, :, :, tc]
            for copy in wind_c():
                copy.start()
        if stage == 4:
            for copy in wind_c():
                copy.wait()
            for i in range(128):
                table[i : i + 1, :] = wc[i // 64, (i // 16) % 4, (i // 4) % 4, i % 4]

    odd_start = z % 2
    first = (7 * z) // 2
    rates[...] = jnp.zeros((8, 1920), F32)
    rates[0:1, 0:BINS] = 0.25 * growth[...]
    rates[1:2, 0:BINS] = 0.25 * dissip[...]
    rates[2:3, 0:50] = speed[...]
    speeds = jnp.broadcast_to(rates[2:3, 0:128], (8, 128))
    speed_high = speeds.astype(BF16)
    speed_mid = (speeds - speed_high.astype(F32)).astype(BF16)
    speed_low = (speeds - speed_high.astype(F32) - speed_mid.astype(F32)).astype(BF16)
    for j in range(5):
        block = first + j
        bins = block * 128 + lax.broadcasted_iota(jnp.int32, (128, 128), 1)
        pick = jnp.where(lax.broadcasted_iota(jnp.int32, (128, 128), 0) == bins % 50, 1.0, 0.0).astype(BF16)
        rate = sum(
            jnp.dot(part, pick, preferred_element_type=F32) for part in (speed_high, speed_mid, speed_low)
        )
        theta = ((bins[0:8] // 50).astype(F32) + 0.5) * (2.0 * math.pi / 36)
        cosine = jnp.abs(jnp.cos(theta))
        sine = jnp.abs(jnp.sin(theta))
        total = cosine + sine
        at = pl.ds(pl.multiple_of(block * 128, 128), 128)
        lines = [
            (rate * cosine / total)[0:1],
            (rate * sine / total)[0:1],
            rates[0:1, at],
            rates[1:2, at],
        ]
        for k, line in enumerate(lines):
            there = pl.ds(pl.multiple_of(128 * j + 64 - 64 * odd_start, 8), 128)
            coef[k, there, :] = jnp.broadcast_to(line, (128, 128)).T

    for load in load_x:
        load.wait()
    load_a.start()
    load_b.start()
    edge = 7 * west
    edge_sea = sea[pl.ds(edge, 1), :]

    def halo_step(i, carry):
        v = take(i, edge)
        halo_out[pl.ds(pl.multiple_of(i * SUB, SUB), SUB), :] = (v * edge_sea).astype(BF16)
        return carry

    lax.fori_loop(0, count, halo_step, 0, unroll=4)
    pl.semaphore_wait(barrier, len(peers))
    halo = pltpu.make_async_remote_copy(
        src_ref=halo_out,
        dst_ref=halo_in,
        send_sem=halo_sem.at[0],
        recv_sem=halo_sem.at[1],
        device_id=(z, lax.rem(t + turn + TILES, TILES)),
        device_id_type=MESH,
    )
    halo.start()
    wind_next(0)
    outer = (1 - west) * (TILES - 1)
    halo_there = (t != outer).astype(F32)

    lane = lax.broadcasted_iota(jnp.int32, (SUB, COLS), 1)
    south = z < 2
    shift = jnp.where(south, 1, COLS - 1)
    wall = lane == jnp.where(south, 0, COLS - 1)
    from_west = west == 1

    def propagate(g, edged):
        r0 = 2 * g
        ru = jnp.clip(r0 + 2 - 3 * west, 0, ROWS - 1)
        sea0 = sea[pl.ds(r0, 1), :]
        sea1 = sea[pl.ds(r0 + 1, 1), :]
        seau = sea[pl.ds(ru, 1), :]
        at_edge = g == (1 - west) * (GROUPS - 1)

        def step(i, carry):
            here = pl.ds(pl.multiple_of(i * SUB, SUB), SUB)
            f0 = take(i, r0) * sea0
            f1 = take(i, r0 + 1) * sea1
            fu = take(i, ru) * seau
            if edged:
                fu = jnp.where(at_edge, halo_in[here, :].astype(F32) * halo_there, fu)
            cx = both(0, i)
            cy = both(1, i)
            up0 = jnp.where(from_west, fu, f1)
            up1 = jnp.where(from_west, f0, fu)
            y0 = jnp.where(wall, 0.0, pltpu.roll(f0, shift, 1))
            y1 = jnp.where(wall, 0.0, pltpu.roll(f1, shift, 1))
            p0 = (f0 - cx * (f0 - up0) - cy * (f0 - y0)) * sea0
            p1 = (f1 - cx * (f1 - up1) - cy * (f1 - y1)) * sea1
            prop[g, here, 0:COLS] = p0
            prop[g, here, COLS:CELLS] = p1
            sent[here, 0:COLS] = p0.astype(BF16)
            sent[here, COLS:CELLS] = p1.astype(BF16)
            return carry

        lax.fori_loop(0, count, step, 0, unroll=4)
        rank = lax.broadcasted_iota(jnp.int32, (cap, COLS), 0).astype(F32)
        onehot[g, :, 0:COLS] = jnp.where(rank == place[pl.ds(r0, 1), :], 1.0, 0.0).astype(BF16)
        onehot[g, :, COLS:CELLS] = jnp.where(rank == place[pl.ds(r0 + 1, 1), :], 1.0, 0.0).astype(BF16)
        return lax.dot_general(sent[...], onehot[g], NT, preferred_element_type=F32).astype(BF16)

    late = z // 3
    early = (3 - z) // 3
    order = [
        1 + lax.rem(z, 2),
        2 * (1 - (z + 2) // 3) + late,
        3 * (1 - late),
    ]

    starts = [sum(parts[:i]) for i in range(len(parts))]

    def forward(i, c):
        return pltpu.make_async_remote_copy(
            src_ref=ahead.at[i, :, pl.ds(starts[c], parts[c])],
            dst_ref=held.at[z, pl.ds(0, WIN), pl.ds(starts[c], parts[c])],
            send_sem=fwd_send.at[c, i],
            recv_sem=fwd_recv.at[c, z],
            device_id=(order[i], t),
            device_id_type=MESH,
        )

    for i in range(2):
        ahead[i] = propagate(order[i], False)
        for c in range(len(parts)):
            forward(i, c).start()

    def keep(mine, block):
        @pl.when(mine)
        def _():
            held[z, 0:WIN, :] = block

        @pl.when(jnp.logical_not(mine))
        def _():
            ahead[2] = block

    keep(z > 0, propagate(z + 3 * early, False))
    wind_next(1)
    halo.wait()
    keep(z == 0, propagate(order[2] * (1 - early), True))
    for c in range(len(parts)):
        forward(2, c).start()
    wind_next(2)
    load_a.wait()
    load_b.wait()

    def returning(i, c):
        h = lax.rem(z + i + 1, 4)
        return pltpu.make_async_remote_copy(
            src_ref=back.at[h, :, pl.ds(starts[c], parts[c])],
            dst_ref=got.at[z, :, pl.ds(starts[c], parts[c])],
            send_sem=ret_send.at[c, i],
            recv_sem=ret_recv.at[c, z],
            device_id=(h, t),
            device_id_type=MESH,
        )

    def landing(c, i):
        g = lax.rem(z + i + 1, 4)
        return pltpu.make_async_remote_copy(
            src_ref=ahead.at[i, :, pl.ds(starts[c], parts[c])],
            dst_ref=held.at[g, pl.ds(0, WIN), pl.ds(starts[c], parts[c])],
            send_sem=fwd_send.at[c, i],
            recv_sem=fwd_recv.at[c, g],
            device_id=(g, t),
            device_id_type=MESH,
        )

    def homing(c, i):
        g = lax.rem(z + i + 1, 4)
        return pltpu.make_async_remote_copy(
            src_ref=back.at[g, :, pl.ds(starts[c], parts[c])],
            dst_ref=got.at[g, :, pl.ds(starts[c], parts[c])],
            send_sem=ret_send.at[c, i],
            recv_sem=ret_recv.at[c, g],
            device_id=(g, t),
            device_id_type=MESH,
        )

    for c, n in enumerate(parts):
        at = pl.ds(starts[c], n)
        for i in range(3):
            landing(c, i).wait_recv()
        if c < 2:
            wind_next(3 + c)
        ones = jnp.ones((SUB, 512), BF16)
        mean = jnp.zeros((SUB, n), F32)
        for s in range(GROUPS):
            block = held[s, :, starts[c] : starts[c] + n]
            mean = mean + jnp.dot(ones, block, preferred_element_type=F32)
            heldt[0:n, 512 * s : 512 * s + 512] = block.T
        mean = mean / BINS
        for k0 in range(0, BINS, 512):
            k1 = min(k0 + 512, BINS)
            sums = []
            for q in (qa, qb):
                acc = None
                for s in range(GROUPS):
                    deep = min(WIN, BINS - STEP * s)
                    term = jnp.dot(
                        heldt[0:n, 512 * s : 512 * s + deep],
                        q[STEP * s : STEP * s + deep, k0:k1],
                        preferred_element_type=F32,
                    )
                    acc = term if acc is None else acc + term
                sums.append(acc)
            pairs[0:n, k0:k1] = (0.25 * (sums[0] * sums[1])).astype(BF16)
        for j in range(15):
            pairst[128 * j : 128 * j + 128, 0:n] = pairs[0:n, 128 * j : 128 * j + 128].T
        row = lax.broadcasted_iota(jnp.int32, (SUB, n), 0)
        high = mean.astype(BF16).astype(F32)
        mid = (mean - high).astype(BF16).astype(F32)
        low = mean - high - mid
        for h in range(GROUPS):
            back[h, 0:STEP, at] = pairst[STEP * h : STEP * h + STEP, 0:n]
            tail = pairst[STEP * h + STEP : STEP * h + WIN, 0:n].astype(F32)
            tail = jnp.where(row == 8, high, tail)
            tail = jnp.where(row == 9, mid, tail)
            tail = jnp.where(row == 10, low, tail)
            back[h, STEP:WIN, at] = tail.astype(BF16)
        for i in range(3):
            returning(i, c).start()

    most[...] = jnp.broadcast_to(jnp.max(table[:, MOST : MOST + 1]), (8, 128))

    wide = table[...]
    w_high = wide.astype(BF16)
    w_mid = (wide - w_high.astype(F32)).astype(BF16)
    w_low = (wide - w_high.astype(F32) - w_mid.astype(F32)).astype(BF16)
    eye = (
        lax.broadcasted_iota(jnp.int32, (MOST, 128), 0) == lax.broadcasted_iota(jnp.int32, (MOST, 128), 1)
    ).astype(F32).astype(BF16)
    tables = [
        lax.dot_general(eye, w, NT, preferred_element_type=F32).astype(BF16) for w in (w_high, w_mid, w_low)
    ]

    def wind_row(r):
        cells = slot[pl.ds(r, 1), :]
        shard = cells // MOST
        line = (shard % 2) * 64 + ((shard // 2) % 4) * 16 + ((shard // 8) % 4) * 4 + shard // 32
        pick = lax.broadcasted_iota(jnp.int32, (128, COLS), 0) == line
        pick = jnp.where(pick, 1.0, 0.0).astype(BF16)
        found = sum(jnp.dot(w, pick, preferred_element_type=F32) for w in tables)
        here = lax.broadcasted_iota(jnp.int32, (MOST, COLS), 0) == cells % MOST
        return jnp.sum(jnp.where(here, found, 0.0), axis=0, keepdims=True)

    def finish(g, source):
        r0 = 2 * g
        inc[...] = jnp.dot(source[g], onehot[g], preferred_element_type=F32)
        means = jnp.sum(inc[STEP + 8 : STEP + 11, :], axis=0, keepdims=True)
        m0 = means[:, 0:COLS]
        m1 = means[:, COLS:CELLS]
        w0 = wind_row(r0)
        w1 = wind_row(r0 + 1)

        def step(i, carry):
            here = pl.ds(pl.multiple_of(i * SUB, SUB), SUB)
            grow = both(2, i)
            damp = both(3, i)
            p0 = prop[g, here, 0:COLS]
            p1 = prop[g, here, COLS:CELLS]
            s0 = p0.astype(BF16).astype(F32)
            s1 = p1.astype(BF16).astype(F32)
            e0 = p0 + inc[here, 0:COLS] + (grow * w0 - damp * m0) * s0
            e1 = p1 + inc[here, COLS:CELLS] + (grow * w1 - damp * m1) * s1
            put(i, r0, e0)
            put(i, r0 + 1, e1)
            return carry

        lax.fori_loop(0, count, step, 0, unroll=4)

    finish(z, back)
    for i in range(3):
        for c in range(len(parts)):
            homing(c, i).wait_recv()
        finish(lax.rem(z + i + 1, 4), got)
    stores = [
        pltpu.make_async_copy(
            field.at[h, pl.ds(2 * z, OWN)], out.at[:, :, pl.ds(128 * h, 128)], load_sem.at[h]
        )
        for h in range(2)
    ]
    for store in stores:
        store.start()
    for i in range(3):
        for c in range(len(parts)):
            forward(i, c).wait_send()
            returning(i, c).wait_send()
    for store in stores:
        store.wait()


def coupled(cap, parts, cid, spectrum, speed, quad_a, quad_b, growth, dissip, wind, slot):
    vmem = pl.BlockSpec(memory_space=pltpu.VMEM)
    hbm = pl.BlockSpec(memory_space=pl.ANY)
    n = len(parts)
    wide = max(parts)
    dma = pltpu.SemaphoreType.DMA
    return pl.pallas_call(
        functools.partial(kernel, cap, parts),
        out_shape=[
            jax.ShapeDtypeStruct(spectrum.shape, F32),
            jax.ShapeDtypeStruct((8, 128), F32),
        ],
        in_specs=[hbm, hbm, hbm, vmem, vmem, vmem, vmem, vmem],
        out_specs=[hbm, vmem],
        scratch_shapes=[
            pltpu.VMEM((2, WIN, ROWS, 128), F32),
            pltpu.VMEM((BINS, BINS), BF16),
            pltpu.VMEM((BINS, BINS), BF16),
            pltpu.VMEM((ROWS, COLS), F32),
            pltpu.VMEM((ROWS, COLS), F32),
            pltpu.VMEM((GROUPS, cap, CELLS), BF16),
            pltpu.VMEM((8, 1920), F32),
            pltpu.VMEM((4, 704, 128), F32),
            pltpu.VMEM((WIN, COLS), BF16),
            pltpu.VMEM((WIN, COLS), BF16),
            pltpu.VMEM((GROUPS, WIN, CELLS), F32),
            pltpu.VMEM((WIN, CELLS), BF16),
            pltpu.VMEM((3, WIN, cap), BF16),
            pltpu.VMEM((GROUPS, 512, cap), BF16),
            pltpu.VMEM((wide, GROUPS * 512), BF16),
            pltpu.VMEM((wide, 1920), BF16),
            pltpu.VMEM((1920, wide), BF16),
            pltpu.VMEM((GROUPS, WIN, cap), BF16),
            pltpu.VMEM((GROUPS, WIN, cap), BF16),
            pltpu.VMEM((WIN, CELLS), F32),
            pltpu.VMEM((4, 4, 2, 1, 128), F32),
            pltpu.VMEM((4, 4, 4, 2, 1, 128), F32),
            pltpu.VMEM((4, 4, 4, 2, 1, 128), F32),
            pltpu.VMEM((2, 4, 4, 4, 1, 128), F32),
            pltpu.VMEM((4, 4, 4, 2, 1, 128), F32),
            pltpu.VMEM((128, 128), F32),
            dma((4,)),
            dma((2,)),
            dma((n, 3)),
            dma((n, 4)),
            dma((n, 3)),
            dma((n, 4)),
            dma((10,)),
            dma((10,)),
        ],
        compiler_params=pltpu.CompilerParams(
            collective_id=cid, has_side_effects=True, vmem_limit_bytes=56 << 20
        ),
        name="coupled%d" % cap,
    )(spectrum, quad_a, quad_b, speed[None], growth[None], dissip[None], wind, slot)


def on_device(spectrum, speed, quad_a, quad_b, growth, dissip, wind, cell_slot):
    inputs = (spectrum, speed, quad_a, quad_b, growth, dissip, wind, cell_slot)
    out, most = coupled(384, (128, 128, 128), 0, *inputs)
    return lax.cond(
        most[0, 0] > 384.0,
        lambda: coupled(CELLS, (128, 128, 128, 128), 1, *inputs)[0],
        lambda: out,
    )


def solution(mesh):
    placed = (
        P("bins", "tiles", None),
        P(),
        P(),
        P(),
        P(),
        P(),
        P(("bins", "tiles"), None),
        P("tiles", None),
    )
    return jax.shard_map(
        on_device, mesh=mesh, in_specs=placed, out_specs=P("bins", "tiles", None), check_vma=False
    )
```

```python
import functools
import math

import jax
import jax.numpy as jnp
from jax import lax
from jax.experimental import pallas as pl
from jax.experimental.pallas import tpu as pltpu
from jax.sharding import PartitionSpec as P

MESH = pl.DeviceIdType.MESH
F32 = jnp.float32
BF16 = jnp.bfloat16

GROUPS = 4
TILES = 32
OWN = 450
STEP = 448
WIN = 464
BINS = 1800
ROWS = 8
COLS = 256
CELLS = 2 * COLS
MOST = 16
SUB = 16
NT = (((1,), (1,)), ((), ()))


def kernel(
    cap,
    parts,
    spec,
    quad_a,
    quad_b,
    speed,
    growth,
    dissip,
    wind,
    slot,
    out,
    most,
    field,
    qa,
    qb,
    sea,
    place,
    onehot,
    rates,
    coef,
    halo_out,
    halo_in,
    prop,
    sent,
    ahead,
    held,
    heldt,
    pairs,
    pairst,
    back,
    got,
    inc,
    wp,
    wy,
    wx,
    wc,
    wz,
    table,
    load_sem,
    halo_sem,
    fwd_send,
    fwd_recv,
    ret_send,
    ret_recv,
    wind_send,
    wind_recv,
):
    z = lax.axis_index("bins")
    t = lax.axis_index("tiles")
    ty = t // 8
    tx = (t // 2) % 4
    tc = t % 2
    west = 1 - ((z + 1) // 2) % 2
    turn = 2 * west - 1
    count = WIN // SUB

    for h in range(2):
        field[h, 0:8] = jnp.zeros((8, ROWS, 128), F32)
        field[h, STEP:WIN] = jnp.zeros((WIN - STEP, ROWS, 128), F32)
    load_x = [
        pltpu.make_async_copy(
            spec.at[:, :, pl.ds(128 * h, 128)], field.at[h, pl.ds(2 * z, OWN)], load_sem.at[h]
        )
        for h in range(2)
    ]
    for load in load_x:
        load.start()
    load_a = pltpu.make_async_copy(quad_a, qa, load_sem.at[2])
    load_b = pltpu.make_async_copy(quad_b, qb, load_sem.at[3])
    barrier = pltpu.get_barrier_semaphore()
    peers = [(lax.rem(z + i, 4), t) for i in (1, 2, 3)]
    peers += [(z, lax.rem(t + 1, TILES)), (z, lax.rem(t + TILES - 1, TILES))]
    ypeers = [lax.rem(ty + i, 4) for i in (1, 2, 3)]
    xpeers = [lax.rem(tx + i, 4) for i in (1, 2, 3)]
    peers += [(z, p * 8 + lax.rem(t, 8)) for p in ypeers]
    peers += [(z, ty * 8 + p * 2 + tc) for p in xpeers]
    for peer in peers:
        pl.semaphore_signal(barrier, inc=1, device_id=peer, device_id_type=MESH)

    wet = (slot[...] >= 0).astype(F32)
    sea[...] = wet
    left = lax.broadcasted_iota(jnp.int32, (COLS, COLS), 0)
    right = lax.broadcasted_iota(jnp.int32, (COLS, COLS), 1)
    upto = (left <= right).astype(F32).astype(BF16)
    running = jnp.dot(wet.astype(BF16), upto, preferred_element_type=F32)
    total = jnp.sum(wet, axis=1, keepdims=True)
    before = pltpu.roll(jnp.broadcast_to(total, (ROWS, COLS)), 1, 0)
    odd = lax.broadcasted_iota(jnp.int32, (ROWS, COLS), 0) % 2 == 1
    running = running + jnp.where(odd, before, 0.0)
    place[...] = jnp.where(wet > 0, running - 1.0, -1.0)
    fullest = jnp.max(running)

    held[:, WIN:512, :] = jnp.zeros((GROUPS, 512 - WIN, cap), BF16)
    pairs[:, 1792:1920] = jnp.zeros((pairs.shape[0], 128), BF16)

    flat = field.reshape(2 * WIN * ROWS, 128)

    def strip(i, r):
        base = i * (SUB * ROWS) + r
        return [pl.ds(h * (WIN * ROWS) + base, SUB, stride=ROWS) for h in range(2)]

    def take(i, r):
        return jnp.concatenate([flat[at, :] for at in strip(i, r)], axis=1)

    def put(i, r, value):
        for h, at in enumerate(strip(i, r)):
            flat[at, :] = value[:, 128 * h : 128 * h + 128]

    def both(k, i):
        one = coef[k, pl.ds(pl.multiple_of(64 + i * SUB, SUB), SUB), :]
        return jnp.concatenate([one, one], axis=1)

    mark = lax.broadcasted_iota(jnp.int32, (1, 128), 1)
    for p in range(TILES):
        row = wind[:, 128 * (p // 8) : 128 * (p // 8) + 128]
        if p % 8:
            row = pltpu.roll(row, 128 - MOST * (p % 8), 1)
        wp[p // 8, (p // 2) % 4, p % 2] = jnp.where(mark == MOST, fullest, row)
    wz[z] = wp[...]

    def wind_copy(k, src, dst, there):
        return pltpu.make_async_remote_copy(
            src_ref=src,
            dst_ref=dst,
            send_sem=wind_send.at[k],
            recv_sem=wind_recv.at[k],
            device_id=there,
            device_id_type=MESH,
        )

    def wind_z():
        return [wind_copy(i, wp, wz.at[z], (lax.rem(z + 1 + i, 4), t)) for i in range(3)]

    def wind_y():
        return [
            wind_copy(3 + i, wz.at[:, p], wy.at[ty], (z, p * 8 + lax.rem(t, 8)))
            for i, p in enumerate(ypeers)
        ]

    def wind_x():
        return [
            wind_copy(6 + i, wy.at[:, :, p], wx.at[tx], (z, ty * 8 + p * 2 + tc))
            for i, p in enumerate(xpeers)
        ]

    def wind_c():
        return [wind_copy(9, wx.at[:, :, :, 1 - tc], wc.at[tc], (z, t + 1 - 2 * tc))]

    def wind_next(stage):
        if stage == 0:
            for copy in wind_z():
                copy.start()
        if stage == 1:
            for copy in wind_z():
                copy.wait()
            wy[ty] = wz[:, ty]
            for copy in wind_y():
                copy.start()
        if stage == 2:
            for copy in wind_y():
                copy.wait()
            wx[tx] = wy[:, :, tx]
            for copy in wind_x():
                copy.start()
        if stage == 3:
            for copy in wind_x():
                copy.wait()
            wc[tc] = wx[:, :, :, tc]
            for copy in wind_c():
                copy.start()
        if stage == 4:
            for copy in wind_c():
                copy.wait()
            for i in range(128):
                table[i : i + 1, :] = wc[i // 64, (i // 16) % 4, (i // 4) % 4, i % 4]

    odd_start = z % 2
    first = (7 * z) // 2
    rates[...] = jnp.zeros((8, 1920), F32)
    rates[0:1, 0:BINS] = 0.25 * growth[...][None]
    rates[1:2, 0:BINS] = 0.25 * dissip[...][None]
    rates[2:3, 0:50] = speed[...][None]
    speeds = jnp.broadcast_to(rates[2:3, 0:128], (8, 128))
    speed_high = speeds.astype(BF16)
    speed_mid = (speeds - speed_high.astype(F32)).astype(BF16)
    speed_low = (speeds - speed_high.astype(F32) - speed_mid.astype(F32)).astype(BF16)
    for j in range(5):
        block = first + j
        bins = block * 128 + lax.broadcasted_iota(jnp.int32, (128, 128), 1)
        pick = jnp.where(lax.broadcasted_iota(jnp.int32, (128, 128), 0) == bins % 50, 1.0, 0.0).astype(BF16)
        rate = sum(
            jnp.dot(part, pick, preferred_element_type=F32) for part in (speed_high, speed_mid, speed_low)
        )
        theta = ((bins[0:8] // 50).astype(F32) + 0.5) * (2.0 * math.pi / 36)
        cosine = jnp.abs(jnp.cos(theta))
        sine = jnp.abs(jnp.sin(theta))
        total = cosine + sine
        at = pl.ds(pl.multiple_of(block * 128, 128), 128)
        lines = [
            (rate * cosine / total)[0:1],
            (rate * sine / total)[0:1],
            rates[0:1, at],
            rates[1:2, at],
        ]
        for k, line in enumerate(lines):
            there = pl.ds(pl.multiple_of(128 * j + 64 - 64 * odd_start, 8), 128)
            coef[k, there, :] = jnp.broadcast_to(line, (128, 128)).T

    for load in load_x:
        load.wait()
    load_a.start()
    load_b.start()
    edge = 7 * west
    edge_sea = sea[pl.ds(edge, 1), :]

    def halo_step(i, carry):
        v = take(i, edge)
        halo_out[pl.ds(pl.multiple_of(i * SUB, SUB), SUB), :] = (v * edge_sea).astype(BF16)
        return carry

    lax.fori_loop(0, count, halo_step, 0, unroll=4)
    pl.semaphore_wait(barrier, len(peers))
    halo = pltpu.make_async_remote_copy(
        src_ref=halo_out,
        dst_ref=halo_in,
        send_sem=halo_sem.at[0],
        recv_sem=halo_sem.at[1],
        device_id=(z, lax.rem(t + turn + TILES, TILES)),
        device_id_type=MESH,
    )
    halo.start()
    wind_next(0)
    outer = (1 - west) * (TILES - 1)
    halo_there = (t != outer).astype(F32)

    lane = lax.broadcasted_iota(jnp.int32, (SUB, COLS), 1)
    south = z < 2
    shift = jnp.where(south, 1, COLS - 1)
    wall = lane == jnp.where(south, 0, COLS - 1)
    from_west = west == 1

    def propagate(g, edged):
        r0 = 2 * g
        ru = jnp.clip(r0 + 2 - 3 * west, 0, ROWS - 1)
        sea0 = sea[pl.ds(r0, 1), :]
        sea1 = sea[pl.ds(r0 + 1, 1), :]
        seau = sea[pl.ds(ru, 1), :]
        at_edge = g == (1 - west) * (GROUPS - 1)

        def step(i, carry):
            here = pl.ds(pl.multiple_of(i * SUB, SUB), SUB)
            f0 = take(i, r0) * sea0
            f1 = take(i, r0 + 1) * sea1
            fu = take(i, ru) * seau
            if edged:
                fu = jnp.where(at_edge, halo_in[here, :].astype(F32) * halo_there, fu)
            cx = both(0, i)
            cy = both(1, i)
            up0 = jnp.where(from_west, fu, f1)
            up1 = jnp.where(from_west, f0, fu)
            y0 = jnp.where(wall, 0.0, pltpu.roll(f0, shift, 1))
            y1 = jnp.where(wall, 0.0, pltpu.roll(f1, shift, 1))
            p0 = (f0 - cx * (f0 - up0) - cy * (f0 - y0)) * sea0
            p1 = (f1 - cx * (f1 - up1) - cy * (f1 - y1)) * sea1
            prop[g, here, 0:COLS] = p0
            prop[g, here, COLS:CELLS] = p1
            sent[here, 0:COLS] = p0.astype(BF16)
            sent[here, COLS:CELLS] = p1.astype(BF16)
            return carry

        lax.fori_loop(0, count, step, 0, unroll=4)
        rank = lax.broadcasted_iota(jnp.int32, (cap, COLS), 0).astype(F32)
        onehot[g, :, 0:COLS] = jnp.where(rank == place[pl.ds(r0, 1), :], 1.0, 0.0).astype(BF16)
        onehot[g, :, COLS:CELLS] = jnp.where(rank == place[pl.ds(r0 + 1, 1), :], 1.0, 0.0).astype(BF16)
        return lax.dot_general(sent[...], onehot[g], NT, preferred_element_type=F32).astype(BF16)

    late = z // 3
    early = (3 - z) // 3
    order = [
        1 + lax.rem(z, 2),
        2 * (1 - (z + 2) // 3) + late,
        3 * (1 - late),
    ]

    starts = [sum(parts[:i]) for i in range(len(parts))]

    def forward(i, c):
        return pltpu.make_async_remote_copy(
            src_ref=ahead.at[i, :, pl.ds(starts[c], parts[c])],
            dst_ref=held.at[z, pl.ds(0, WIN), pl.ds(starts[c], parts[c])],
            send_sem=fwd_send.at[c, i],
            recv_sem=fwd_recv.at[c, z],
            device_id=(order[i], t),
            device_id_type=MESH,
        )

    for i in range(2):
        ahead[i] = propagate(order[i], False)
        for c in range(len(parts)):
            forward(i, c).start()

    def keep(mine, block):
        @pl.when(mine)
        def _():
            held[z, 0:WIN, :] = block

        @pl.when(jnp.logical_not(mine))
        def _():
            ahead[2] = block

    keep(z > 0, propagate(z + 3 * early, False))
    wind_next(1)
    halo.wait()
    keep(z == 0, propagate(order[2] * (1 - early), True))
    for c in range(len(parts)):
        forward(2, c).start()
    wind_next(2)
    load_a.wait()
    load_b.wait()

    def returning(i, c):
        h = lax.rem(z + i + 1, 4)
        return pltpu.make_async_remote_copy(
            src_ref=back.at[h, :, pl.ds(starts[c], parts[c])],
            dst_ref=got.at[z, :, pl.ds(starts[c], parts[c])],
            send_sem=ret_send.at[c, i],
            recv_sem=ret_recv.at[c, z],
            device_id=(h, t),
            device_id_type=MESH,
        )

    def landing(c, i):
        g = lax.rem(z + i + 1, 4)
        return pltpu.make_async_remote_copy(
            src_ref=ahead.at[i, :, pl.ds(starts[c], parts[c])],
            dst_ref=held.at[g, pl.ds(0, WIN), pl.ds(starts[c], parts[c])],
            send_sem=fwd_send.at[c, i],
            recv_sem=fwd_recv.at[c, g],
            device_id=(g, t),
            device_id_type=MESH,
        )

    def homing(c, i):
        g = lax.rem(z + i + 1, 4)
        return pltpu.make_async_remote_copy(
            src_ref=back.at[g, :, pl.ds(starts[c], parts[c])],
            dst_ref=got.at[g, :, pl.ds(starts[c], parts[c])],
            send_sem=ret_send.at[c, i],
            recv_sem=ret_recv.at[c, g],
            device_id=(g, t),
            device_id_type=MESH,
        )

    for c, n in enumerate(parts):
        at = pl.ds(starts[c], n)
        for i in range(3):
            landing(c, i).wait_recv()
        if c < 2:
            wind_next(3 + c)
        ones = jnp.ones((SUB, 512), BF16)
        mean = jnp.zeros((SUB, n), F32)
        for s in range(GROUPS):
            block = held[s, :, starts[c] : starts[c] + n]
            mean = mean + jnp.dot(ones, block, preferred_element_type=F32)
            heldt[0:n, 512 * s : 512 * s + 512] = block.T
        mean = mean / BINS
        for k0 in range(0, BINS, 512):
            k1 = min(k0 + 512, BINS)
            sums = []
            for q in (qa, qb):
                acc = None
                for s in range(GROUPS):
                    deep = min(WIN, BINS - STEP * s)
                    term = jnp.dot(
                        heldt[0:n, 512 * s : 512 * s + deep],
                        q[STEP * s : STEP * s + deep, k0:k1],
                        preferred_element_type=F32,
                    )
                    acc = term if acc is None else acc + term
                sums.append(acc)
            pairs[0:n, k0:k1] = (0.25 * (sums[0] * sums[1])).astype(BF16)
        for j in range(15):
            pairst[128 * j : 128 * j + 128, 0:n] = pairs[0:n, 128 * j : 128 * j + 128].T
        row = lax.broadcasted_iota(jnp.int32, (SUB, n), 0)
        high = mean.astype(BF16).astype(F32)
        mid = (mean - high).astype(BF16).astype(F32)
        low = mean - high - mid
        for h in range(GROUPS):
            back[h, 0:STEP, at] = pairst[STEP * h : STEP * h + STEP, 0:n]
            tail = pairst[STEP * h + STEP : STEP * h + WIN, 0:n].astype(F32)
            tail = jnp.where(row == 8, high, tail)
            tail = jnp.where(row == 9, mid, tail)
            tail = jnp.where(row == 10, low, tail)
            back[h, STEP:WIN, at] = tail.astype(BF16)
        for i in range(3):
            returning(i, c).start()

    most[0] = (jnp.max(table[:, MOST : MOST + 1]) > cap).astype(jnp.int32)

    wide = table[...]
    w_high = wide.astype(BF16)
    w_mid = (wide - w_high.astype(F32)).astype(BF16)
    w_low = (wide - w_high.astype(F32) - w_mid.astype(F32)).astype(BF16)
    eye = (
        lax.broadcasted_iota(jnp.int32, (MOST, 128), 0) == lax.broadcasted_iota(jnp.int32, (MOST, 128), 1)
    ).astype(F32).astype(BF16)
    tables = [
        lax.dot_general(eye, w, NT, preferred_element_type=F32).astype(BF16) for w in (w_high, w_mid, w_low)
    ]

    def wind_row(r):
        cells = slot[pl.ds(r, 1), :]
        shard = cells // MOST
        line = (shard % 2) * 64 + ((shard // 2) % 4) * 16 + ((shard // 8) % 4) * 4 + shard // 32
        pick = lax.broadcasted_iota(jnp.int32, (128, COLS), 0) == line
        pick = jnp.where(pick, 1.0, 0.0).astype(BF16)
        found = sum(jnp.dot(w, pick, preferred_element_type=F32) for w in tables)
        here = lax.broadcasted_iota(jnp.int32, (MOST, COLS), 0) == cells % MOST
        return jnp.sum(jnp.where(here, found, 0.0), axis=0, keepdims=True)

    def finish(g, source):
        r0 = 2 * g
        inc[...] = jnp.dot(source[g], onehot[g], preferred_element_type=F32)
        means = jnp.sum(inc[STEP + 8 : STEP + 11, :], axis=0, keepdims=True)
        m0 = means[:, 0:COLS]
        m1 = means[:, COLS:CELLS]
        w0 = wind_row(r0)
        w1 = wind_row(r0 + 1)

        def step(i, carry):
            here = pl.ds(pl.multiple_of(i * SUB, SUB), SUB)
            grow = both(2, i)
            damp = both(3, i)
            p0 = prop[g, here, 0:COLS]
            p1 = prop[g, here, COLS:CELLS]
            s0 = p0.astype(BF16).astype(F32)
            s1 = p1.astype(BF16).astype(F32)
            e0 = p0 + inc[here, 0:COLS] + (grow * w0 - damp * m0) * s0
            e1 = p1 + inc[here, COLS:CELLS] + (grow * w1 - damp * m1) * s1
            put(i, r0, e0)
            put(i, r0 + 1, e1)
            return carry

        lax.fori_loop(0, count, step, 0, unroll=4)

    finish(z, back)
    for i in range(3):
        for c in range(len(parts)):
            homing(c, i).wait_recv()
        finish(lax.rem(z + i + 1, 4), got)
    for h in range(2):
        out[:, :, 128 * h : 128 * h + 128] = field[h, pl.ds(2 * z, OWN)]
    for i in range(3):
        for c in range(len(parts)):
            forward(i, c).wait_send()
            returning(i, c).wait_send()


def coupled(cap, parts, cid, spectrum, speed, quad_a, quad_b, growth, dissip, wind, slot):
    vmem = pl.BlockSpec(memory_space=pltpu.VMEM)
    hbm = pl.BlockSpec(memory_space=pl.ANY)
    n = len(parts)
    wide = max(parts)
    dma = pltpu.SemaphoreType.DMA
    return pl.pallas_call(
        functools.partial(kernel, cap, parts),
        out_shape=[
            pltpu.VMEM(spectrum.shape, F32),
            jax.ShapeDtypeStruct((1,), jnp.int32),
        ],
        in_specs=[hbm, hbm, hbm, vmem, vmem, vmem, vmem, vmem],
        out_specs=[vmem, pl.BlockSpec(memory_space=pltpu.SMEM)],
        scratch_shapes=[
            pltpu.VMEM((2, WIN, ROWS, 128), F32),
            pltpu.VMEM((BINS, BINS), BF16),
            pltpu.VMEM((BINS, BINS), BF16),
            pltpu.VMEM((ROWS, COLS), F32),
            pltpu.VMEM((ROWS, COLS), F32),
            pltpu.VMEM((GROUPS, cap, CELLS), BF16),
            pltpu.VMEM((8, 1920), F32),
            pltpu.VMEM((4, 704, 128), F32),
            pltpu.VMEM((WIN, COLS), BF16),
            pltpu.VMEM((WIN, COLS), BF16),
            pltpu.VMEM((GROUPS, WIN, CELLS), F32),
            pltpu.VMEM((WIN, CELLS), BF16),
            pltpu.VMEM((3, WIN, cap), BF16),
            pltpu.VMEM((GROUPS, 512, cap), BF16),
            pltpu.VMEM((wide, GROUPS * 512), BF16),
            pltpu.VMEM((wide, 1920), BF16),
            pltpu.VMEM((1920, wide), BF16),
            pltpu.VMEM((GROUPS, WIN, cap), BF16),
            pltpu.VMEM((GROUPS, WIN, cap), BF16),
            pltpu.VMEM((WIN, CELLS), F32),
            pltpu.VMEM((4, 4, 2, 1, 128), F32),
            pltpu.VMEM((4, 4, 4, 2, 1, 128), F32),
            pltpu.VMEM((4, 4, 4, 2, 1, 128), F32),
            pltpu.VMEM((2, 4, 4, 4, 1, 128), F32),
            pltpu.VMEM((4, 4, 4, 2, 1, 128), F32),
            pltpu.VMEM((128, 128), F32),
            dma((4,)),
            dma((2,)),
            dma((n, 3)),
            dma((n, 4)),
            dma((n, 3)),
            dma((n, 4)),
            dma((10,)),
            dma((10,)),
        ],
        compiler_params=pltpu.CompilerParams(
            collective_id=cid, has_side_effects=True, vmem_limit_bytes=56 << 20
        ),
        name="coupled%d" % cap,
    )(spectrum, quad_a, quad_b, speed, growth, dissip, wind, slot)


def on_device(spectrum, speed, quad_a, quad_b, growth, dissip, wind, cell_slot):
    inputs = (spectrum, speed, quad_a, quad_b, growth, dissip, wind, cell_slot)
    out, most = coupled(384, (128, 128, 128), 0, *inputs)
    out = lax.cond(
        most[0] != 0,
        lambda: coupled(CELLS, (128, 128, 128, 128), 1, *inputs)[0],
        lambda: out,
    )
    return out


def solution(mesh):
    placed = (
        P("bins", "tiles", None),
        P(),
        P(),
        P(),
        P(),
        P(),
        P(("bins", "tiles"), None),
        P("tiles", None),
    )
    return jax.shard_map(
        on_device, mesh=mesh, in_specs=placed, out_specs=P("bins", "tiles", None), check_vma=False
    )
```

```python
import functools
import math

import jax
import jax.numpy as jnp
from jax import lax
from jax.experimental import pallas as pl
from jax.experimental.pallas import tpu as pltpu
from jax.sharding import PartitionSpec as P

MESH = pl.DeviceIdType.MESH
F32 = jnp.float32
BF16 = jnp.bfloat16

GROUPS = 4
TILES = 32
OWN = 450
STEP = 448
WIN = 464
BINS = 1800
ROWS = 8
COLS = 256
CELLS = 2 * COLS
MOST = 16
SUB = 16
NT = (((1,), (1,)), ((), ()))


def kernel(
    cap,
    parts,
    spec,
    quad_a,
    quad_b,
    speed,
    growth,
    dissip,
    wind,
    slot,
    out,
    most,
    field,
    qa,
    qb,
    sea,
    place,
    onehot,
    rates,
    coef,
    halo_out,
    halo_in,
    prop,
    sent,
    ahead,
    held,
    heldt,
    pairs,
    pairst,
    back,
    got,
    inc,
    wp,
    wy,
    wx,
    wc,
    wz,
    table,
    winds,
    load_sem,
    halo_sem,
    fwd_send,
    fwd_recv,
    ret_send,
    ret_recv,
    wind_send,
    wind_recv,
):
    z = lax.axis_index("bins")
    t = lax.axis_index("tiles")
    ty = t // 8
    tx = (t // 2) % 4
    tc = t % 2
    west = 1 - ((z + 1) // 2) % 2
    turn = 2 * west - 1
    count = WIN // SUB

    for h in range(2):
        field[h, 0:8] = jnp.zeros((8, ROWS, 128), F32)
        field[h, STEP:WIN] = jnp.zeros((WIN - STEP, ROWS, 128), F32)
    load_x = [
        pltpu.make_async_copy(
            spec.at[:, :, pl.ds(128 * h, 128)], field.at[h, pl.ds(2 * z, OWN)], load_sem.at[h]
        )
        for h in range(2)
    ]
    for load in load_x:
        load.start()
    load_a = pltpu.make_async_copy(quad_a, qa, load_sem.at[2])
    load_b = pltpu.make_async_copy(quad_b, qb, load_sem.at[3])
    barrier = pltpu.get_barrier_semaphore()
    peers = [(lax.rem(z + i, 4), t) for i in (1, 2, 3)]
    peers += [(z, lax.rem(t + 1, TILES)), (z, lax.rem(t + TILES - 1, TILES))]
    ypeers = [lax.rem(ty + i, 4) for i in (1, 2, 3)]
    xpeers = [lax.rem(tx + i, 4) for i in (1, 2, 3)]
    peers += [(z, p * 8 + lax.rem(t, 8)) for p in ypeers]
    peers += [(z, ty * 8 + p * 2 + tc) for p in xpeers]
    for peer in peers:
        pl.semaphore_signal(barrier, inc=1, device_id=peer, device_id_type=MESH)

    wet = (slot[...] >= 0).astype(F32)
    sea[...] = wet
    left = lax.broadcasted_iota(jnp.int32, (COLS, COLS), 0)
    right = lax.broadcasted_iota(jnp.int32, (COLS, COLS), 1)
    upto = (left <= right).astype(F32).astype(BF16)
    running = jnp.dot(wet.astype(BF16), upto, preferred_element_type=F32)
    total = jnp.sum(wet, axis=1, keepdims=True)
    before = pltpu.roll(jnp.broadcast_to(total, (ROWS, COLS)), 1, 0)
    odd = lax.broadcasted_iota(jnp.int32, (ROWS, COLS), 0) % 2 == 1
    running = running + jnp.where(odd, before, 0.0)
    place[...] = jnp.where(wet > 0, running - 1.0, -1.0)
    fullest = jnp.max(running)

    held[:, WIN:512, :] = jnp.zeros((GROUPS, 512 - WIN, cap), BF16)
    pairs[:, 1792:1920] = jnp.zeros((pairs.shape[0], 128), BF16)

    flat = field.reshape(2 * WIN * ROWS, 128)

    def strip(i, r):
        base = i * (SUB * ROWS) + r
        return [pl.ds(h * (WIN * ROWS) + base, SUB, stride=ROWS) for h in range(2)]

    def take(i, r):
        return jnp.concatenate([flat[at, :] for at in strip(i, r)], axis=1)

    def put(i, r, value):
        for h, at in enumerate(strip(i, r)):
            flat[at, :] = value[:, 128 * h : 128 * h + 128]

    def both(k, i):
        one = coef[k, pl.ds(pl.multiple_of(64 + i * SUB, SUB), SUB), :]
        return jnp.concatenate([one, one], axis=1)

    def wind_copy(k, src, dst, there):
        return pltpu.make_async_remote_copy(
            src_ref=src,
            dst_ref=dst,
            send_sem=wind_send.at[k],
            recv_sem=wind_recv.at[k],
            device_id=there,
            device_id_type=MESH,
        )

    def wind_z():
        return [wind_copy(i, wp, wz.at[z], (lax.rem(z + 1 + i, 4), t)) for i in range(3)]

    def wind_y():
        return [
            wind_copy(3 + i, wz.at[:, p], wy.at[ty], (z, p * 8 + lax.rem(t, 8)))
            for i, p in enumerate(ypeers)
        ]

    def wind_x():
        return [
            wind_copy(6 + i, wy.at[:, :, p], wx.at[tx], (z, ty * 8 + p * 2 + tc))
            for i, p in enumerate(xpeers)
        ]

    def wind_c():
        return [wind_copy(9, wx.at[:, :, :, 1 - tc], wc.at[tc], (z, t + 1 - 2 * tc))]

    def wind_next(stage):
        if stage == 0:
            for copy in wind_z():
                copy.start()
        if stage == 1:
            for copy in wind_z():
                copy.wait()
            wy[ty] = wz[:, ty]
            for copy in wind_y():
                copy.start()
        if stage == 2:
            for copy in wind_y():
                copy.wait()
            wx[tx] = wy[:, :, tx]
            for copy in wind_x():
                copy.start()
        if stage == 3:
            for copy in wind_x():
                copy.wait()
            wc[tc] = wx[:, :, :, tc]
            for copy in wind_c():
                copy.start()
        if stage == 4:
            for copy in wind_c():
                copy.wait()
            for i in range(128):
                table[i : i + 1, :] = wc[i // 64, (i // 16) % 4, (i // 4) % 4, i % 4]

    odd_start = z % 2
    first = (7 * z) // 2
    rates[...] = jnp.zeros((8, 1920), F32)
    rates[0:1, 0:BINS] = 0.25 * growth[...][None]
    rates[1:2, 0:BINS] = 0.25 * dissip[...][None]
    rates[2:3, 0:50] = speed[...][None]
    speeds = jnp.broadcast_to(rates[2:3, 0:128], (8, 128))
    speed_high = speeds.astype(BF16)
    speed_mid = (speeds - speed_high.astype(F32)).astype(BF16)
    speed_low = (speeds - speed_high.astype(F32) - speed_mid.astype(F32)).astype(BF16)

    def columns(k, j, line):
        there = pl.ds(pl.multiple_of(128 * j + 64 - 64 * odd_start, 8), 128)
        coef[k, there, :] = jnp.broadcast_to(line, (128, 128)).T

    for j in range(5):
        block = first + j
        bins = block * 128 + lax.broadcasted_iota(jnp.int32, (128, 128), 1)
        pick = jnp.where(lax.broadcasted_iota(jnp.int32, (128, 128), 0) == bins % 50, 1.0, 0.0).astype(BF16)
        rate = sum(
            jnp.dot(part, pick, preferred_element_type=F32) for part in (speed_high, speed_mid, speed_low)
        )
        theta = ((bins[0:8] // 50).astype(F32) + 0.5) * (2.0 * math.pi / 36)
        cosine = jnp.abs(jnp.cos(theta))
        sine = jnp.abs(jnp.sin(theta))
        total = cosine + sine
        columns(0, j, (rate * cosine / total)[0:1])
        columns(1, j, (rate * sine / total)[0:1])

    for load in load_x:
        load.wait()
    load_a.start()
    load_b.start()
    edge = 7 * west
    edge_sea = sea[pl.ds(edge, 1), :]

    def halo_step(i, carry):
        v = take(i, edge)
        halo_out[pl.ds(pl.multiple_of(i * SUB, SUB), SUB), :] = (v * edge_sea).astype(BF16)
        return carry

    lax.fori_loop(0, count, halo_step, 0, unroll=4)
    pl.semaphore_wait(barrier, len(peers))
    halo = pltpu.make_async_remote_copy(
        src_ref=halo_out,
        dst_ref=halo_in,
        send_sem=halo_sem.at[0],
        recv_sem=halo_sem.at[1],
        device_id=(z, lax.rem(t + turn + TILES, TILES)),
        device_id_type=MESH,
    )
    halo.start()
    mark = lax.broadcasted_iota(jnp.int32, (1, 128), 1)
    for p in range(TILES):
        row = wind[:, 128 * (p // 8) : 128 * (p // 8) + 128]
        if p % 8:
            row = pltpu.roll(row, 128 - MOST * (p % 8), 1)
        wp[p // 8, (p // 2) % 4, p % 2] = jnp.where(mark == MOST, fullest, row)
    wz[z] = wp[...]
    wind_next(0)
    outer = (1 - west) * (TILES - 1)
    halo_there = (t != outer).astype(F32)

    lane = lax.broadcasted_iota(jnp.int32, (SUB, COLS), 1)
    south = z < 2
    shift = jnp.where(south, 1, COLS - 1)
    wall = lane == jnp.where(south, 0, COLS - 1)
    from_west = west == 1

    def propagate(g, edged):
        r0 = 2 * g
        ru = jnp.clip(r0 + 2 - 3 * west, 0, ROWS - 1)
        sea0 = sea[pl.ds(r0, 1), :]
        sea1 = sea[pl.ds(r0 + 1, 1), :]
        seau = sea[pl.ds(ru, 1), :]
        at_edge = g == (1 - west) * (GROUPS - 1)

        def step(i, carry):
            here = pl.ds(pl.multiple_of(i * SUB, SUB), SUB)
            f0 = take(i, r0) * sea0
            f1 = take(i, r0 + 1) * sea1
            fu = take(i, ru) * seau
            if edged:
                fu = jnp.where(at_edge, halo_in[here, :].astype(F32) * halo_there, fu)
            cx = both(0, i)
            cy = both(1, i)
            up0 = jnp.where(from_west, fu, f1)
            up1 = jnp.where(from_west, f0, fu)
            y0 = jnp.where(wall, 0.0, pltpu.roll(f0, shift, 1))
            y1 = jnp.where(wall, 0.0, pltpu.roll(f1, shift, 1))
            p0 = (f0 - cx * (f0 - up0) - cy * (f0 - y0)) * sea0
            p1 = (f1 - cx * (f1 - up1) - cy * (f1 - y1)) * sea1
            prop[g, here, 0:COLS] = p0
            prop[g, here, COLS:CELLS] = p1
            sent[here, 0:COLS] = p0.astype(BF16)
            sent[here, COLS:CELLS] = p1.astype(BF16)
            return carry

        lax.fori_loop(0, count, step, 0, unroll=4)
        rank = lax.broadcasted_iota(jnp.int32, (cap, COLS), 0).astype(F32)
        onehot[g, :, 0:COLS] = jnp.where(rank == place[pl.ds(r0, 1), :], 1.0, 0.0).astype(BF16)
        onehot[g, :, COLS:CELLS] = jnp.where(rank == place[pl.ds(r0 + 1, 1), :], 1.0, 0.0).astype(BF16)
        return lax.dot_general(sent[...], onehot[g], NT, preferred_element_type=F32).astype(BF16)

    late = z // 3
    early = (3 - z) // 3
    order = [
        1 + lax.rem(z, 2),
        2 * (1 - (z + 2) // 3) + late,
        3 * (1 - late),
    ]

    starts = [sum(parts[:i]) for i in range(len(parts))]

    def forward(i, c):
        return pltpu.make_async_remote_copy(
            src_ref=ahead.at[i, :, pl.ds(starts[c], parts[c])],
            dst_ref=held.at[z, pl.ds(0, WIN), pl.ds(starts[c], parts[c])],
            send_sem=fwd_send.at[c, i],
            recv_sem=fwd_recv.at[c, z],
            device_id=(order[i], t),
            device_id_type=MESH,
        )

    for i in range(2):
        ahead[i] = propagate(order[i], False)
        for c in range(len(parts)):
            forward(i, c).start()

    def keep(mine, block):
        @pl.when(mine)
        def _():
            held[z, 0:WIN, :] = block

        @pl.when(jnp.logical_not(mine))
        def _():
            ahead[2] = block

    keep(z > 0, propagate(z + 3 * early, False))
    halo.wait()
    keep(z == 0, propagate(order[2] * (1 - early), True))
    for c in range(len(parts)):
        forward(2, c).start()
    wind_next(1)
    for j in range(5):
        at = pl.ds(pl.multiple_of((first + j) * 128, 128), 128)
        columns(2, j, rates[0:1, at])
        columns(3, j, rates[1:2, at])
    load_a.wait()
    load_b.wait()
    wind_next(2)

    def returning(i, c):
        h = lax.rem(z + i + 1, 4)
        return pltpu.make_async_remote_copy(
            src_ref=back.at[h, :, pl.ds(starts[c], parts[c])],
            dst_ref=got.at[z, :, pl.ds(starts[c], parts[c])],
            send_sem=ret_send.at[c, i],
            recv_sem=ret_recv.at[c, z],
            device_id=(h, t),
            device_id_type=MESH,
        )

    def landing(c, i):
        g = lax.rem(z + i + 1, 4)
        return pltpu.make_async_remote_copy(
            src_ref=ahead.at[i, :, pl.ds(starts[c], parts[c])],
            dst_ref=held.at[g, pl.ds(0, WIN), pl.ds(starts[c], parts[c])],
            send_sem=fwd_send.at[c, i],
            recv_sem=fwd_recv.at[c, g],
            device_id=(g, t),
            device_id_type=MESH,
        )

    def homing(c, i):
        g = lax.rem(z + i + 1, 4)
        return pltpu.make_async_remote_copy(
            src_ref=back.at[g, :, pl.ds(starts[c], parts[c])],
            dst_ref=got.at[g, :, pl.ds(starts[c], parts[c])],
            send_sem=ret_send.at[c, i],
            recv_sem=ret_recv.at[c, g],
            device_id=(g, t),
            device_id_type=MESH,
        )

    for c, n in enumerate(parts):
        at = pl.ds(starts[c], n)
        for i in range(3):
            landing(c, i).wait_recv()
        if c < 2:
            wind_next(3 + c)
        ones = jnp.ones((SUB, 512), BF16)
        mean = jnp.zeros((SUB, n), F32)
        for s in range(GROUPS):
            block = held[s, :, starts[c] : starts[c] + n]
            mean = mean + jnp.dot(ones, block, preferred_element_type=F32)
            heldt[0:n, 512 * s : 512 * s + 512] = block.T
        mean = mean / BINS
        for k0 in range(0, BINS, 512):
            k1 = min(k0 + 512, BINS)
            sums = []
            for q in (qa, qb):
                acc = None
                for s in range(GROUPS):
                    deep = min(WIN, BINS - STEP * s)
                    term = jnp.dot(
                        heldt[0:n, 512 * s : 512 * s + deep],
                        q[STEP * s : STEP * s + deep, k0:k1],
                        preferred_element_type=F32,
                    )
                    acc = term if acc is None else acc + term
                sums.append(acc)
            pairs[0:n, k0:k1] = (0.25 * (sums[0] * sums[1])).astype(BF16)
        for j in range(15):
            pairst[128 * j : 128 * j + 128, 0:n] = pairs[0:n, 128 * j : 128 * j + 128].T
        row = lax.broadcasted_iota(jnp.int32, (SUB, n), 0)
        high = mean.astype(BF16).astype(F32)
        mid = (mean - high).astype(BF16).astype(F32)
        low = mean - high - mid
        for h in range(GROUPS):
            back[h, 0:STEP, at] = pairst[STEP * h : STEP * h + STEP, 0:n]
            tail = pairst[STEP * h + STEP : STEP * h + WIN, 0:n].astype(F32)
            tail = jnp.where(row == 8, high, tail)
            tail = jnp.where(row == 9, mid, tail)
            tail = jnp.where(row == 10, low, tail)
            back[h, STEP:WIN, at] = tail.astype(BF16)
        for i in range(3):
            returning(i, c).start()

    most[0] = (jnp.max(table[:, MOST : MOST + 1]) > cap).astype(jnp.int32)

    wide = table[...]
    w_high = wide.astype(BF16)
    w_mid = (wide - w_high.astype(F32)).astype(BF16)
    w_low = (wide - w_high.astype(F32) - w_mid.astype(F32)).astype(BF16)
    eye = (
        lax.broadcasted_iota(jnp.int32, (MOST, 128), 0) == lax.broadcasted_iota(jnp.int32, (MOST, 128), 1)
    ).astype(F32).astype(BF16)
    tables = [
        lax.dot_general(eye, w, NT, preferred_element_type=F32).astype(BF16) for w in (w_high, w_mid, w_low)
    ]

    def wind_row(r):
        cells = slot[pl.ds(r, 1), :]
        shard = cells // MOST
        line = (shard % 2) * 64 + ((shard // 2) % 4) * 16 + ((shard // 8) % 4) * 4 + shard // 32
        pick = lax.broadcasted_iota(jnp.int32, (128, COLS), 0) == line
        pick = jnp.where(pick, 1.0, 0.0).astype(BF16)
        found = sum(jnp.dot(w, pick, preferred_element_type=F32) for w in tables)
        here = lax.broadcasted_iota(jnp.int32, (MOST, COLS), 0) == cells % MOST
        return jnp.sum(jnp.where(here, found, 0.0), axis=0, keepdims=True)

    def finish(g, source):
        r0 = 2 * g
        inc[...] = jnp.dot(source[g], onehot[g], preferred_element_type=F32)
        means = jnp.sum(inc[STEP + 8 : STEP + 11, :], axis=0, keepdims=True)
        m0 = means[:, 0:COLS]
        m1 = means[:, COLS:CELLS]
        w0 = winds[pl.ds(r0, 1), :]
        w1 = winds[pl.ds(r0 + 1, 1), :]

        def step(i, carry):
            here = pl.ds(pl.multiple_of(i * SUB, SUB), SUB)
            grow = both(2, i)
            damp = both(3, i)
            p0 = prop[g, here, 0:COLS]
            p1 = prop[g, here, COLS:CELLS]
            s0 = p0.astype(BF16).astype(F32)
            s1 = p1.astype(BF16).astype(F32)
            e0 = p0 + inc[here, 0:COLS] + (grow * w0 - damp * m0) * s0
            e1 = p1 + inc[here, COLS:CELLS] + (grow * w1 - damp * m1) * s1
            put(i, r0, e0)
            put(i, r0 + 1, e1)
            return carry

        lax.fori_loop(0, count, step, 0, unroll=4)

    for r in range(ROWS):
        winds[r : r + 1, :] = wind_row(r)
    finish(z, back)
    for i in (0, 2, 1):
        for c in range(len(parts)):
            homing(c, i).wait_recv()
        finish(lax.rem(z + i + 1, 4), got)
    for h in range(2):
        out[:, :, 128 * h : 128 * h + 128] = field[h, pl.ds(2 * z, OWN)]
    for i in range(3):
        for c in range(len(parts)):
            forward(i, c).wait_send()
            returning(i, c).wait_send()


def coupled(cap, parts, cid, spectrum, speed, quad_a, quad_b, growth, dissip, wind, slot):
    vmem = pl.BlockSpec(memory_space=pltpu.VMEM)
    hbm = pl.BlockSpec(memory_space=pl.ANY)
    n = len(parts)
    wide = max(parts)
    dma = pltpu.SemaphoreType.DMA
    return pl.pallas_call(
        functools.partial(kernel, cap, parts),
        out_shape=[
            pltpu.VMEM(spectrum.shape, F32),
            jax.ShapeDtypeStruct((1,), jnp.int32),
        ],
        in_specs=[hbm, hbm, hbm, vmem, vmem, vmem, vmem, vmem],
        out_specs=[vmem, pl.BlockSpec(memory_space=pltpu.SMEM)],
        scratch_shapes=[
            pltpu.VMEM((2, WIN, ROWS, 128), F32),
            pltpu.VMEM((BINS, BINS), BF16),
            pltpu.VMEM((BINS, BINS), BF16),
            pltpu.VMEM((ROWS, COLS), F32),
            pltpu.VMEM((ROWS, COLS), F32),
            pltpu.VMEM((GROUPS, cap, CELLS), BF16),
            pltpu.VMEM((8, 1920), F32),
            pltpu.VMEM((4, 704, 128), F32),
            pltpu.VMEM((WIN, COLS), BF16),
            pltpu.VMEM((WIN, COLS), BF16),
            pltpu.VMEM((GROUPS, WIN, CELLS), F32),
            pltpu.VMEM((WIN, CELLS), BF16),
            pltpu.VMEM((3, WIN, cap), BF16),
            pltpu.VMEM((GROUPS, 512, cap), BF16),
            pltpu.VMEM((wide, GROUPS * 512), BF16),
            pltpu.VMEM((wide, 1920), BF16),
            pltpu.VMEM((1920, wide), BF16),
            pltpu.VMEM((GROUPS, WIN, cap), BF16),
            pltpu.VMEM((GROUPS, WIN, cap), BF16),
            pltpu.VMEM((WIN, CELLS), F32),
            pltpu.VMEM((4, 4, 2, 1, 128), F32),
            pltpu.VMEM((4, 4, 4, 2, 1, 128), F32),
            pltpu.VMEM((4, 4, 4, 2, 1, 128), F32),
            pltpu.VMEM((2, 4, 4, 4, 1, 128), F32),
            pltpu.VMEM((4, 4, 4, 2, 1, 128), F32),
            pltpu.VMEM((128, 128), F32),
            pltpu.VMEM((ROWS, COLS), F32),
            dma((4,)),
            dma((2,)),
            dma((n, 3)),
            dma((n, 4)),
            dma((n, 3)),
            dma((n, 4)),
            dma((10,)),
            dma((10,)),
        ],
        compiler_params=pltpu.CompilerParams(
            collective_id=cid, has_side_effects=True, vmem_limit_bytes=56 << 20
        ),
        name="coupled%d" % cap,
    )(spectrum, quad_a, quad_b, speed, growth, dissip, wind, slot)


def on_device(spectrum, speed, quad_a, quad_b, growth, dissip, wind, cell_slot):
    inputs = (spectrum, speed, quad_a, quad_b, growth, dissip, wind, cell_slot)
    out, most = coupled(384, (128, 128, 128), 0, *inputs)
    out = lax.cond(
        most[0] != 0,
        lambda: coupled(CELLS, (128, 128, 128, 128), 1, *inputs)[0],
        lambda: out,
    )
    return out


def solution(mesh):
    placed = (
        P("bins", "tiles", None),
        P(),
        P(),
        P(),
        P(),
        P(),
        P(("bins", "tiles"), None),
        P("tiles", None),
    )
    return jax.shard_map(
        on_device, mesh=mesh, in_specs=placed, out_specs=P("bins", "tiles", None), check_vma=False
    )
```
